32 devices in a mesh: section: 2 (over x), seq: 4 (over z), fsdp: 4 (over y, core).
Axes of the slice: x: 2, y: 2, z: 4, core: 2. Of those that a mesh axis runs over, the one named last changes fastest.
Arguments:
- inputs: bfloat16 [2, 4, 1024, 768], P(None, 'fsdp', 'seq'), may hold values from -6 to 6
- cotangent: bfloat16 [2, 4, 1024, 768], P(None, 'fsdp', 'seq'), may hold values from -6 to 6
- w_qkv: bfloat16 [2, 768, 2304], P('section', 'fsdp'), may hold values from -0.21875 to 0.21875
- w_attn_out: bfloat16 [2, 768, 768], P('section', 'fsdp'), may hold values from -2.5 to 2.5
- w_in: bfloat16 [2, 768, 2304], P('section', 'fsdp'), may hold values from -0.21875 to 0.21875
- w_ff_out: bfloat16 [2, 1152, 768], P('section', 'fsdp'), may hold values from -0.1875 to 0.1875
- ln_attn: bfloat16 [2, 768], P('section', 'fsdp'), may hold values from 0.5 to 1.5
- ln_ff: bfloat16 [2, 768], P('section', 'fsdp'), may hold values from 0.5 to 1.5
Outputs:
- layer_out: bfloat16 [2, 2, 4, 1024, 768], P('section', None, 'fsdp', 'seq')
- in_grad: float32 [2, 2, 4, 1024, 768], P('section', None, 'fsdp', 'seq')
- g_qkv: float32 [2, 768, 2304], P('section', 'fsdp')
- g_attn_out: float32 [2, 768, 768], P('section', 'fsdp')
- g_in: float32 [2, 768, 2304], P('section', 'fsdp')
- g_ff_out: float32 [2, 1152, 768], P('section', 'fsdp')
- g_ln_attn: float32 [2, 768], P('section', 'fsdp')
- g_ln_ff: float32 [2, 768], P('section', 'fsdp')
The draws below stay inside these ranges and needn't reach their ends.
All inputs are finite; a program needn't handle non-finite values.
Results may differ from the reference program's by a relative error of at most 0.023.
Values may be sent and summed in bfloat16 or wider, within the bound.
A program may use at most 128 MiB of HBM per device.

```python
import math
import jax
import jax.numpy as jnp
from jax import lax

D = 768
HEADS = 12
HEAD_DIM = 64
FF = 1152
HALF = 64
MICRO = 2
LENGTH = 1024
SEQS = 4


def steps_of(stream_key, extent, split, least, high):
    factor_of, own = 1.0, jax.random.fold_in(stream_key, 6)
    for position, shards_of in split:
        draws = jnp.exp(jax.random.uniform(jax.random.fold_in(own, position), (shards_of,), jnp.float32, least / len(split), high / len(split)))
        factor_of = factor_of * jnp.repeat(draws, extent[position] // shards_of).reshape([-1 if axis == position else 1 for axis in range(len(extent))])
    return factor_of


def normal_values(own_key, extent, scale, reach, cuts=(), kind=jnp.bfloat16):
    values = scale * jax.random.normal(own_key, extent, jnp.float32)
    if cuts:
        values = values * steps_of(own_key, extent, cuts, -0.22, 0.18)
    return jnp.clip(values, -reach, reach).astype(kind)


def setup_inputs(seed: int = 0) -> dict:
    streams_of = jax.random.split(jax.random.key(seed), 9)
    return {
        "inputs": normal_values(streams_of[0], (MICRO, SEQS, LENGTH, D), 1.0, 6.0, ((1, 4), (2, 4))),
        "cotangent": normal_values(streams_of[1], (MICRO, SEQS, LENGTH, D), 1.0, 6.0, ((1, 4), (2, 4))),
        "w_qkv": normal_values(streams_of[2], (2, D, 3 * D), D ** -0.5, 0.21875, ((0, 2), (1, 4))),
        "w_attn_out": normal_values(streams_of[3], (2, D, D), (D // (2 * HALF)) ** -0.5, 2.5, ((0, 2), (1, 4))),
        "w_in": normal_values(streams_of[4], (2, D, 2 * FF), D ** -0.5, 0.21875, ((0, 2), (1, 4))),
        "w_ff_out": normal_values(streams_of[5], (2, FF, D), FF ** -0.5, 0.1875, ((0, 2), (1, 4))),
        "ln_attn": jnp.clip(1.0 + 0.1 * jax.random.normal(streams_of[6], (2, D), jnp.float32), 0.5, 1.5).astype(jnp.bfloat16),
        "ln_ff": jnp.clip(1.0 + 0.1 * jax.random.normal(streams_of[7], (2, D), jnp.float32), 0.5, 1.5).astype(jnp.bfloat16),
    }


@jax.custom_vjp
def low(v):
    return lax.optimization_barrier(v.astype(jnp.bfloat16)).astype(jnp.float32)

@jax.custom_vjp
def low_back(v):
    return v

def low_keep(v):
    return (low(v), None)

def low_pass(kept, grad):
    return (grad,)

def back_keep(v):
    return (v, None)

def back_low(kept, grad):
    return (low(grad),)
low.defvjp(low_keep, low_pass)
low_back.defvjp(back_keep, back_low)

def matmul(left, right):
    return jnp.dot(left, right, precision=lax.Precision.HIGHEST)

def layer_norm(values, gain):
    centre = values - lax.optimization_barrier(jnp.mean(values, axis=-1, keepdims=True))
    spread = lax.optimization_barrier(jnp.mean(centre * centre, axis=-1, keepdims=True))
    return centre * lax.rsqrt(spread + 1e-05) * gain

def layer(weights, values):
    mat_qkv, mat_out, mat_in, mat_ff, gain_attn, gain_ff = weights
    length = values.shape[0]
    normed = low(layer_norm(values, gain_attn))
    projected = low_back(low(matmul(normed, mat_qkv)))
    query_rows = projected[:, :D]
    key_pad = jnp.pad(projected[:, D:2 * D], ((HALF, HALF), (0, 0)))
    value_pad = jnp.pad(projected[:, 2 * D:], ((HALF, HALF), (0, 0)))
    block_len = math.gcd(length, 512)
    span = block_len + 2 * HALF

    def attend(start):
        query_block = lax.dynamic_slice_in_dim(query_rows, start, block_len, 0).reshape(block_len, HEADS, HEAD_DIM)
        key_block = lax.dynamic_slice_in_dim(key_pad, start, span, 0).reshape(span, HEADS, HEAD_DIM)
        value_block = lax.dynamic_slice_in_dim(value_pad, start, span, 0).reshape(span, HEADS, HEAD_DIM)
        scores = jnp.einsum('qhd,khd->hqk', query_block, key_block, precision=lax.Precision.HIGHEST) * HEAD_DIM ** (-0.5)
        scores = low_back(scores)
        query_pos = start + jnp.arange(block_len, dtype=jnp.int32)[:, None]
        key_pos = start + jnp.arange(span, dtype=jnp.int32)[None, :] - HALF
        allowed = (jnp.abs(key_pos - query_pos) <= HALF) & (key_pos >= 0) & (key_pos < length)
        probs = jax.nn.softmax(jnp.where(allowed[None], scores, -1e+30), axis=-1)
        mixed = jnp.einsum('hqk,khd->qhd', low(probs), value_block, precision=lax.Precision.HIGHEST)
        return mixed.reshape(block_len, D)
    starts = jnp.arange(length // block_len, dtype=jnp.int32) * block_len
    attended = lax.map(jax.checkpoint(attend), starts).reshape(length, D)
    attended = low_back(low(attended))
    hidden_in = values + low_back(matmul(attended, mat_out))
    normed_ff = low(layer_norm(hidden_in, gain_ff))
    gate_up = low_back(matmul(normed_ff, mat_in))
    hidden = low(jax.nn.gelu(gate_up[:, :FF], approximate=False) * gate_up[:, FF:])
    return hidden_in + low_back(matmul(hidden, mat_ff))

def two_layers(params, values, probe):
    first = low(layer(tuple((param[0] for param in params)), values))
    carried = low_back(first + probe)
    return (first, low(layer(tuple((param[1] for param in params)), carried)))

def whole(params, sequences, probes):

    def advance(unused, sequence_pair):
        return (unused, jax.checkpoint(two_layers)(params, sequence_pair[0], sequence_pair[1]))
    unused, result = lax.scan(advance, jnp.zeros((), jnp.float32), (sequences, probes))
    return result

def reference(inputs, cotangent, w_qkv, w_attn_out, w_in, w_ff_out, ln_attn, ln_ff):
    params = tuple((arr.astype(jnp.float32) for arr in (w_qkv, w_attn_out, w_in, w_ff_out, ln_attn, ln_ff)))
    sequences = inputs.astype(jnp.float32).reshape(MICRO * SEQS, LENGTH, D)
    probes = jnp.zeros_like(sequences)
    result, backward = jax.vjp(whole, params, sequences, probes)
    firsts, lasts = result
    seeds = (jnp.zeros_like(firsts), cotangent.astype(jnp.float32).reshape(MICRO * SEQS, LENGTH, D))
    grad_params, grad_inputs, grad_probes = backward(seeds)
    layer_out = jnp.stack([firsts, lasts]).reshape(2, MICRO, SEQS, LENGTH, D).astype(jnp.bfloat16)
    in_grad = jnp.stack([grad_inputs, grad_probes]).reshape(2, MICRO, SEQS, LENGTH, D)
    return (layer_out, in_grad, grad_params[0], grad_params[1], grad_params[2], grad_params[3], grad_params[4], grad_params[5])
```

```python
import functools

import jax
import jax.numpy as jnp
from jax import lax
from jax.experimental import pallas as pl
from jax.experimental.pallas import tpu as pltpu
from jax.sharding import PartitionSpec as P

D = 768
HEAD_DIM = 64
FF = 1152
HALF = 64
PAIRS = D // 128
EPS = 1e-05
SCALE = HEAD_DIM ** (-0.5)
BF = jnp.bfloat16
F32 = jnp.float32
VMEM_LIMIT = 56 * 1024 * 1024
ANY = pl.BlockSpec(memory_space=pl.ANY)
VM = pl.BlockSpec(memory_space=pltpu.VMEM)


def dot_nn(x, y):
    return lax.dot_general(x, y, (((1,), (0,)), ((), ())), preferred_element_type=F32)


def dot_nt(x, y):
    return lax.dot_general(x, y, (((1,), (1,)), ((), ())), preferred_element_type=F32)


def dot_tn(x, y):
    return lax.dot_general(x, y, (((0,), (0,)), ((), ())), preferred_element_type=F32)


def normed_rows(v):
    centre = v - jnp.mean(v, axis=-1, keepdims=True)
    inv = lax.rsqrt(jnp.mean(centre * centre, axis=-1, keepdims=True) + EPS)
    return centre * inv, inv


def norm_back(grad, n, inv, gain):
    e = grad * gain
    return inv * (e - jnp.mean(e, axis=-1, keepdims=True) - n * jnp.mean(e * n, axis=-1, keepdims=True))


def two_heads(x):
    lane = lax.broadcasted_iota(jnp.int32, x.shape, 1)
    zero = jnp.zeros_like(x)
    return jnp.concatenate([jnp.where(lane < 64, x, zero), jnp.where(lane < 64, zero, x)], axis=0)


def one_of_two(x):
    rows = x.shape[0] // 2
    lane = lax.broadcasted_iota(jnp.int32, (rows, 128), 1)
    return jnp.where(lane < 64, x[:rows], x[rows:])


def allowed_mask(qb, start, seq_idx, seq_count, block_rows):
    shape = (2 * qb, qb + 2 * HALF)
    row = lax.broadcasted_iota(jnp.int32, shape, 0)
    row = jnp.where(row >= qb, row - qb, row)
    col = lax.broadcasted_iota(jnp.int32, shape, 1)
    rel = col - row
    key = seq_idx * block_rows + start - HALF + col
    return (rel >= 0) & (rel <= 2 * HALF) & (key >= 0) & (key < seq_count * block_rows)


def probs_of(q2, k, mask):
    scores = jnp.where(mask, dot_nt(q2, k) * SCALE, -1e30)
    expo = jnp.exp(scores - jnp.max(scores, axis=-1, keepdims=True))
    return expo / jnp.sum(expo, axis=-1, keepdims=True)


def forward_kernel(has_own, has_recv, seq_count, *refs):
    refs = list(refs)
    own = refs.pop(0) if has_own else None
    recv = [refs.pop(0) for _ in range(3)] if has_recv else None
    (gain_a, gain_f, w_qkv, w_out, w_in, w_ff, u_out, qkv_ref, o_ref, h_ref, gu_ref, out_ref,
     s_qkv, s_out, s_in, s_ff, sems) = refs
    copies = [pltpu.make_async_copy(src, dst, sems.at[i]) for i, (src, dst) in
              enumerate(((w_qkv, s_qkv), (w_out, s_out), (w_in, s_in), (w_ff, s_ff)))]
    for copy in copies:
        copy.start()
    rows = out_ref.shape[0]
    sec = lax.axis_index("section")
    seq_idx = lax.axis_index("seq")
    if has_recv:
        u_b = jnp.concatenate([recv[1][...], recv[0][...], recv[2][...]], axis=0)
        if has_own:
            pick = (jnp.zeros(u_b.shape, jnp.int32) + sec) == 0
            u_f = jnp.where(pick, own[...].astype(F32), u_b.astype(F32))
            u_b = u_f.astype(BF)
    else:
        u_b = own[...]
    u_out[...] = u_b
    u = u_b.astype(F32)
    a = (normed_rows(u)[0] * gain_a[...]).astype(BF)
    copies[0].wait()
    qkv_ref[...] = dot_nn(a, s_qkv[...]).astype(BF)
    qb = min(rows, 128)
    for start in range(0, rows, qb):
        mask = allowed_mask(qb, start, seq_idx, seq_count, rows)
        span = slice(start, start + qb + 2 * HALF)
        for p in range(PAIRS):
            lanes = slice(p * 128, p * 128 + 128)
            q2 = two_heads(qkv_ref[HALF + start:HALF + start + qb, lanes])
            k = qkv_ref[span, D + p * 128:D + p * 128 + 128]
            v = qkv_ref[span, 2 * D + p * 128:2 * D + p * 128 + 128]
            mixed = dot_nn(probs_of(q2, k, mask).astype(BF), v)
            o_ref[start:start + qb, lanes] = one_of_two(mixed).astype(BF)
    copies[1].wait()
    h = u_out[HALF:HALF + rows].astype(F32) + dot_nn(o_ref[...], s_out[...])
    h_ref[...] = h
    b = (normed_rows(h)[0] * gain_f[...]).astype(BF)
    copies[2].wait()
    gu_ref[...] = dot_nn(b, s_in[...])
    gate = gu_ref[:, :FF]
    hid = (0.5 * gate * (1.0 + lax.erf(gate * 0.7071067811865476)) * gu_ref[:, FF:]).astype(BF)
    copies[3].wait()
    out_ref[...] = (h_ref[...] + dot_nn(hid, s_ff[...])).astype(BF)


WEIGHT_SCRATCH = [
    pltpu.VMEM((D, 3 * D), BF),
    pltpu.VMEM((D, D), BF),
    pltpu.VMEM((D, 2 * FF), BF),
    pltpu.VMEM((FF, D), BF),
]


def forward_call(own, recv, gains, mats, rows, seq_count):
    ext = rows + 2 * HALF
    args = ([own] if own is not None else []) + (list(recv) if recv is not None else [])
    shape = jax.ShapeDtypeStruct
    return pl.pallas_call(
        functools.partial(forward_kernel, own is not None, recv is not None, seq_count),
        out_shape=(shape((ext, D), BF), shape((ext, 3 * D), BF), shape((rows, D), BF),
                   shape((rows, D), F32), shape((rows, 2 * FF), F32), shape((rows, D), BF)),
        in_specs=[VM] * (len(args) + 2) + [ANY] * 4,
        out_specs=(VM,) * 6,
        scratch_shapes=WEIGHT_SCRATCH + [pltpu.SemaphoreType.DMA((4,))],
        compiler_params=pltpu.CompilerParams(vmem_limit_bytes=VMEM_LIMIT),
    )(*args, *gains, *mats)


def backward_kernel(has_cot, has_recv, same, seq_count, *refs):
    refs = list(refs)
    cot = refs.pop(0) if has_cot else None
    recv = [refs.pop(0) for _ in range(3)] if has_recv else None
    gain_a, gain_f = refs[:2]
    weights = refs[2:6]
    refs = refs[6:]
    kept_a, refs = refs[:5], refs[5:]
    kept_b, refs = refs[:5], refs[5:]
    (du_ref, du_b_ref, rim_ref, a_ref, dqkv_ref, o_out, dattn_ref, b_ref, dgu_ref, hid_ref, dff_ref,
     ga_ref, gf_ref) = refs[:13]
    s_qkv, s_out, s_in, s_ff, u_s, qkv_s, h_s, gu_s, dout, do_s, acc, sems = refs[13:]
    kept_s = (u_s, qkv_s, o_out, h_s, gu_s)
    rows = du_ref.shape[0]
    ext = rows + 2 * HALF
    sec = lax.axis_index("section")
    seq_idx = lax.axis_index("seq")

    @pl.when(sec == 0)
    def _():
        for i in (4, 3, 0, 1, 2):
            pltpu.make_async_copy(kept_a[i], kept_s[i], sems.at[4 + i]).start()

    @pl.when(sec != 0)
    def _():
        for i in (4, 3, 0, 1, 2):
            pltpu.make_async_copy(kept_b[i], kept_s[i], sems.at[4 + i]).start()

    kept_copies = [pltpu.make_async_copy(kept_a[i], kept_s[i], sems.at[4 + i]) for i in range(5)]
    copies = [pltpu.make_async_copy(src, dst, sems.at[i]) for i, (src, dst) in
              enumerate(zip(weights, (s_qkv, s_out, s_in, s_ff)))]
    for i in (3, 2, 1, 0):
        copies[i].start()
    if has_recv:
        dout[...] = recv[0][...].astype(F32)
        dout[0:HALF] += recv[1][...].astype(F32)
        dout[rows - HALF:rows] += recv[2][...].astype(F32)
        got = dout[...].astype(BF).astype(F32)
    else:
        got = jnp.zeros((rows, D), F32)
    if has_cot:
        pick = (jnp.zeros((rows, D), jnp.int32) + sec) == 1
        got = jnp.where(pick, cot[...].astype(F32), got)
    dout[...] = got
    dff_ref[...] = got.astype(BF)
    copies[3].wait()
    dhid = dot_nt(dff_ref[...], s_ff[...])
    kept_copies[4].wait()
    gate, up = gu_s[:, :FF], gu_s[:, FF:]
    cdf = 0.5 * (1.0 + lax.erf(gate * 0.7071067811865476))
    act = gate * cdf
    hid_ref[...] = (act * up).astype(BF)
    pdf = jnp.exp(-0.5 * gate * gate) * 0.3989422804014327
    dgu_ref[:, :FF] = (dhid * up * (cdf + gate * pdf)).astype(BF)
    dgu_ref[:, FF:] = (dhid * act).astype(BF)
    copies[2].wait()
    db = dot_nt(dgu_ref[...], s_in[...])
    kept_copies[3].wait()
    n, inv = normed_rows(h_s[...])
    b_ref[...] = (n * gain_f[...]).astype(BF)
    gf_ref[...] = jnp.sum(db * n, axis=0, keepdims=True)
    dout[...] += norm_back(db, n, inv, gain_f[...])
    dattn_ref[...] = dout[...].astype(BF)
    copies[1].wait()
    do_s[...] = dot_nt(dattn_ref[...], s_out[...]).astype(BF)
    kept_copies[0].wait()
    kept_copies[1].wait()
    kept_copies[2].wait()
    acc[...] = jnp.zeros_like(acc)
    dqkv_ref[0:HALF, 0:D] = jnp.zeros((HALF, D), BF)
    dqkv_ref[ext - HALF:ext, 0:D] = jnp.zeros((HALF, D), BF)
    qb = min(rows, 128)
    for start in range(0, rows, qb):
        mask = allowed_mask(qb, start, seq_idx, seq_count, rows)
        span = slice(start, start + qb + 2 * HALF)
        mid = slice(HALF + start, HALF + start + qb)
        for p in range(PAIRS):
            lanes = slice(p * 128, p * 128 + 128)
            klanes = slice(D + p * 128, D + p * 128 + 128)
            vlanes = slice(2 * D + p * 128, 2 * D + p * 128 + 128)
            q2 = two_heads(qkv_s[mid, lanes])
            k = qkv_s[span, klanes]
            v = qkv_s[span, vlanes]
            do2 = two_heads(do_s[start:start + qb, lanes])
            probs = probs_of(q2, k, mask)
            dp = dot_nt(do2, v)
            ds = (probs * (dp - jnp.sum(probs * dp, axis=-1, keepdims=True))).astype(BF)
            dqkv_ref[mid, lanes] = (one_of_two(dot_nn(ds, k)) * SCALE).astype(BF)
            acc[span, lanes] += dot_tn(ds, q2) * SCALE
            acc[span, klanes] += dot_tn(probs.astype(BF), do2)
    dqkv_ref[:, D:] = acc[...].astype(BF)
    copies[0].wait()
    da = dot_nt(dqkv_ref[...], s_qkv[...])
    m, inv_u = normed_rows(u_s[...].astype(F32))
    a_ref[...] = (m * gain_a[...]).astype(BF)
    ga_ref[...] = jnp.sum(da * m, axis=0, keepdims=True)
    du = norm_back(da, m, inv_u, gain_a[...])
    rim_ref[0:HALF] = du[:HALF].astype(BF)
    rim_ref[HALF:2 * HALF] = du[ext - HALF:].astype(BF)
    du_mid = dout[...] + du[HALF:HALF + rows]
    du_ref[...] = du_mid
    du_b_ref[...] = du_mid.astype(BF)


def backward_call(cot, recv, gains, mats, kept_a, kept_b, rows, seq_count):
    ext = rows + 2 * HALF
    args = ([cot] if cot is not None else []) + (list(recv) if recv is not None else [])
    shape = jax.ShapeDtypeStruct
    return pl.pallas_call(
        functools.partial(backward_kernel, cot is not None, recv is not None, False, seq_count),
        out_shape=(shape((rows, D), F32), shape((rows, D), BF), shape((2 * HALF, D), BF), shape((ext, D), BF),
                   shape((ext, 3 * D), BF), shape((rows, D), BF), shape((rows, D), BF),
                   shape((rows, D), BF), shape((rows, 2 * FF), BF), shape((rows, FF), BF),
                   shape((rows, D), BF), shape((1, D), F32), shape((1, D), F32)),
        in_specs=[VM] * (len(args) + 2) + [ANY] * 14,
        out_specs=(VM,) * 13,
        scratch_shapes=WEIGHT_SCRATCH + [
            pltpu.VMEM((ext, D), BF), pltpu.VMEM((ext, 3 * D), BF), pltpu.VMEM((rows, D), F32),
            pltpu.VMEM((rows, 2 * FF), F32), pltpu.VMEM((rows, D), F32), pltpu.VMEM((rows, D), BF),
            pltpu.VMEM((ext, 2 * D), F32), pltpu.SemaphoreType.DMA((9,)),
        ],
        compiler_params=pltpu.CompilerParams(vmem_limit_bytes=VMEM_LIMIT),
    )(*args, *gains, *mats, *kept_a, *kept_b)


def weight_kernel(*refs):
    slots = (refs[0:8], refs[8:16], refs[16:24])
    outs = refs[24:28]
    bufs = refs[28:36]
    sems = refs[36]
    sec = lax.axis_index("section")
    order = (6, 7, 4, 5, 2, 3, 0, 1)

    def copy(slot, i, part):
        rows = slots[slot][i].shape[0]
        return pltpu.make_async_copy(slots[slot][i], bufs[i].at[pl.ds(part * rows, rows)],
                                     sems.at[part, i])

    for i in order:
        copy(1, i, 0).start()

        @pl.when(sec == 0)
        def _():
            copy(2, i, 1).start()

        @pl.when(sec != 0)
        def _():
            copy(0, i, 1).start()

    for w in (3, 2, 1, 0):
        for i in (2 * w, 2 * w + 1):
            copy(1, i, 0).wait()
            copy(2, i, 1).wait()
        left = bufs[2 * w][...]
        width = outs[w].shape[1]
        step = 384
        for c in range(0, width, step):
            outs[w][:, c:c + step] = dot_tn(left, bufs[2 * w + 1][:, c:c + step]).astype(BF)


def weight_call(slots):
    shape = jax.ShapeDtypeStruct
    scratch = [pltpu.VMEM((2 * x.shape[0], x.shape[1]), BF) for x in slots[0]]
    return pl.pallas_call(
        weight_kernel,
        out_shape=(shape((D, 3 * D), BF), shape((D, D), BF), shape((D, 2 * FF), BF), shape((FF, D), BF)),
        in_specs=[ANY] * 24,
        out_specs=(VM,) * 4,
        scratch_shapes=scratch + [pltpu.SemaphoreType.DMA((2, 8))],
        compiler_params=pltpu.CompilerParams(vmem_limit_bytes=VMEM_LIMIT),
    )(*slots[0], *slots[1], *slots[2])


def neighbours(seq_count, from_sec, to_sec, by):
    return [(from_sec * seq_count + i, to_sec * seq_count + i + by)
            for i in range(seq_count) if 0 <= i + by < seq_count]


def body(inputs, cotangent, w_qkv, w_attn_out, w_in, w_ff_out, ln_attn, ln_ff):
    sec = lax.axis_index("section")
    seq_count = lax.axis_size("seq")
    rows = inputs.shape[2]
    axes = ("section", "seq")
    x = inputs[:, 0]
    right = [(i, i + 1) for i in range(seq_count - 1)]
    left = [(i + 1, i) for i in range(seq_count - 1)]
    from_left = lax.ppermute(x[:, rows - HALF:], "seq", right)
    from_right = lax.ppermute(x[:, :HALF], "seq", left)
    own = jnp.concatenate([from_left, x, from_right], axis=1)
    mats = tuple(lax.all_gather(w[0], "fsdp", axis=0, tiled=True) for w in (w_qkv, w_attn_out, w_in, w_ff_out))
    gains = lax.all_gather(jnp.concatenate([ln_attn, ln_ff], axis=0), "fsdp", axis=1, tiled=True).astype(F32)
    gains = (gains[0:1], gains[1:2])

    def relay(out):
        return (
            lax.ppermute(out, "section", [(0, 1)]),
            lax.ppermute(out[rows - HALF:], axes, neighbours(seq_count, 0, 1, 1)),
            lax.ppermute(out[:HALF], axes, neighbours(seq_count, 0, 1, -1)),
        )

    def relay_back(du_b, rim):
        return (
            lax.ppermute(du_b, "section", [(1, 0)]),
            lax.ppermute(rim[HALF:], axes, neighbours(seq_count, 1, 0, 1)),
            lax.ppermute(rim[:HALF], axes, neighbours(seq_count, 1, 0, -1)),
        )

    kept0 = forward_call(own[0], None, gains, mats, rows, seq_count)
    kept1 = forward_call(own[1], relay(kept0[5]), gains, mats, rows, seq_count)
    kept2 = forward_call(None, relay(kept1[5]), gains, mats, rows, seq_count)
    kept = [k[:5] for k in (kept0, kept1, kept2)]
    cot = cotangent[:, 0]
    back0 = backward_call(cot[0], None, gains, mats, kept[0], kept[1], rows, seq_count)
    back1 = backward_call(cot[1], relay_back(back0[1], back0[2]), gains, mats, kept[0], kept[2], rows, seq_count)
    back2 = backward_call(None, relay_back(back1[1], back1[2]), gains, mats, kept[1], kept[2], rows, seq_count)
    backs = (back0, back1, back2)
    rims = jnp.where(sec == 0, jnp.stack([back1[2], back2[2]]), jnp.stack([back0[2], back1[2]]))
    to_right = lax.ppermute(rims[:, HALF:], "seq", right).astype(F32)
    to_left = lax.ppermute(rims[:, :HALF], "seq", left).astype(F32)
    totals = weight_call([b[3:11] for b in backs])
    ln_totals = jnp.concatenate([sum(b[11] for b in backs), sum(b[12] for b in backs)], axis=0)
    owned = tuple(lax.psum_scatter(t, "fsdp", scatter_dimension=0, tiled=True) for t in totals)
    owned_ln = lax.psum_scatter(ln_totals.astype(BF), "fsdp", scatter_dimension=1, tiled=True)
    summed = lax.psum(owned + (owned_ln,), "seq")
    summed = tuple(s.astype(F32) for s in summed)
    layer_out = jnp.where(sec == 0, jnp.stack([kept0[5], kept1[5]]), jnp.stack([kept1[5], kept2[5]]))
    grad = jnp.where(sec == 0, jnp.stack([back1[0], back2[0]]), jnp.stack([back0[0], back1[0]]))
    pad = ((0, 0), (0, rows - HALF), (0, 0))
    grad = grad + jnp.pad(to_right, pad)
    grad = grad + jnp.pad(to_left, (pad[0], pad[1][::-1], pad[2]))
    grad = jnp.where(sec == 1, grad.astype(BF).astype(F32), grad)
    return (layer_out[None, :, None], grad[None, :, None], summed[0][None], summed[1][None], summed[2][None],
            summed[3][None], summed[4][0:1], summed[4][1:2])


def solution(mesh):
    placed = (
        P(None, "fsdp", "seq", None),
        P(None, "fsdp", "seq", None),
        P("section", "fsdp", None),
        P("section", "fsdp", None),
        P("section", "fsdp", None),
        P("section", "fsdp", None),
        P("section", "fsdp"),
        P("section", "fsdp"),
    )
    return jax.shard_map(
        body,
        mesh=mesh,
        in_specs=placed,
        out_specs=(
            P("section", None, "fsdp", "seq", None),
            P("section", None, "fsdp", "seq", None),
            P("section", "fsdp", None),
            P("section", "fsdp", None),
            P("section", "fsdp", None),
            P("section", "fsdp", None),
            P("section", "fsdp"),
            P("section", "fsdp"),
        ),
        check_vma=False,
    )
```

```python
import functools

import jax
import jax.numpy as jnp
from jax import lax
from jax.experimental import pallas as pl
from jax.experimental.pallas import tpu as pltpu
from jax.sharding import PartitionSpec as P

D = 768
HEAD_DIM = 64
FF = 1152
HALF = 64
PAIRS = D // 128
EPS = 1e-05
SCALE = HEAD_DIM ** (-0.5)
BF = jnp.bfloat16
F32 = jnp.float32
VMEM_LIMIT = 56 * 1024 * 1024
ANY = pl.BlockSpec(memory_space=pl.ANY)
VM = pl.BlockSpec(memory_space=pltpu.VMEM)


def dot_nn(x, y):
    return lax.dot_general(x, y, (((1,), (0,)), ((), ())), preferred_element_type=F32)


def dot_nt(x, y):
    return lax.dot_general(x, y, (((1,), (1,)), ((), ())), preferred_element_type=F32)


def dot_tn(x, y):
    return lax.dot_general(x, y, (((0,), (0,)), ((), ())), preferred_element_type=F32)


def normed_rows(v):
    centre = v - jnp.mean(v, axis=-1, keepdims=True)
    inv = lax.rsqrt(jnp.mean(centre * centre, axis=-1, keepdims=True) + EPS)
    return centre * inv, inv


def norm_back(grad, n, inv, gain):
    e = grad * gain
    return inv * (e - jnp.mean(e, axis=-1, keepdims=True) - n * jnp.mean(e * n, axis=-1, keepdims=True))


def two_heads(x):
    lane = lax.broadcasted_iota(jnp.int32, x.shape, 1)
    zero = jnp.zeros_like(x)
    return jnp.concatenate([jnp.where(lane < 64, x, zero), jnp.where(lane < 64, zero, x)], axis=0)


def one_of_two(x):
    rows = x.shape[0] // 2
    lane = lax.broadcasted_iota(jnp.int32, (rows, 128), 1)
    return jnp.where(lane < 64, x[:rows], x[rows:])


def allowed_mask(qb, start, seq_idx, seq_count, block_rows):
    shape = (2 * qb, qb + 2 * HALF)
    row = lax.broadcasted_iota(jnp.int32, shape, 0)
    row = jnp.where(row >= qb, row - qb, row)
    col = lax.broadcasted_iota(jnp.int32, shape, 1)
    rel = col - row
    key = seq_idx * block_rows + start - HALF + col
    return (rel >= 0) & (rel <= 2 * HALF) & (key >= 0) & (key < seq_count * block_rows)


def probs_of(q2, k, mask):
    scores = jnp.where(mask, dot_nt(q2, k) * SCALE, -1e30)
    expo = jnp.exp(scores - jnp.max(scores, axis=-1, keepdims=True))
    return expo / jnp.sum(expo, axis=-1, keepdims=True)


def forward_kernel(has_own, has_recv, seq_count, *refs):
    refs = list(refs)
    own = refs.pop(0) if has_own else None
    recv = [refs.pop(0) for _ in range(3)] if has_recv else None
    (gain_a, gain_f, w_qkv, w_out, w_in, w_ff, u_out, qkv_ref, o_ref, h_ref, gu_ref, out_ref,
     s_qkv, s_out, s_in, s_ff, sems) = refs
    copies = [pltpu.make_async_copy(src, dst, sems.at[i]) for i, (src, dst) in
              enumerate(((w_qkv, s_qkv), (w_out, s_out), (w_in, s_in), (w_ff, s_ff)))]
    for copy in copies:
        copy.start()
    rows = out_ref.shape[0]
    sec = lax.axis_index("section")
    seq_idx = lax.axis_index("seq")
    if has_recv:
        u_b = jnp.concatenate([recv[1][...], recv[0][...], recv[2][...]], axis=0)
        if has_own:
            pick = (jnp.zeros(u_b.shape, jnp.int32) + sec) == 0
            u_f = jnp.where(pick, own[...].astype(F32), u_b.astype(F32))
            u_b = u_f.astype(BF)
    else:
        u_b = own[...]
    u_out[...] = u_b
    u = u_b.astype(F32)
    a = (normed_rows(u)[0] * gain_a[...]).astype(BF)
    copies[0].wait()
    qkv_ref[...] = dot_nn(a, s_qkv[...]).astype(BF)
    qb = min(rows, 128)
    for start in range(0, rows, qb):
        mask = allowed_mask(qb, start, seq_idx, seq_count, rows)
        span = slice(start, start + qb + 2 * HALF)
        for p in range(PAIRS):
            lanes = slice(p * 128, p * 128 + 128)
            q2 = two_heads(qkv_ref[HALF + start:HALF + start + qb, lanes])
            k = qkv_ref[span, D + p * 128:D + p * 128 + 128]
            v = qkv_ref[span, 2 * D + p * 128:2 * D + p * 128 + 128]
            mixed = dot_nn(probs_of(q2, k, mask).astype(BF), v)
            o_ref[start:start + qb, lanes] = one_of_two(mixed).astype(BF)
    copies[1].wait()
    h = u_out[HALF:HALF + rows].astype(F32) + dot_nn(o_ref[...], s_out[...])
    h_ref[...] = h
    b = (normed_rows(h)[0] * gain_f[...]).astype(BF)
    copies[2].wait()
    gu_ref[...] = dot_nn(b, s_in[...])
    gate = gu_ref[:, :FF]
    hid = (0.5 * gate * (1.0 + lax.erf(gate * 0.7071067811865476)) * gu_ref[:, FF:]).astype(BF)
    copies[3].wait()
    out_ref[...] = (h_ref[...] + dot_nn(hid, s_ff[...])).astype(BF)


WEIGHT_SCRATCH = [
    pltpu.VMEM((D, 3 * D), BF),
    pltpu.VMEM((D, D), BF),
    pltpu.VMEM((D, 2 * FF), BF),
    pltpu.VMEM((FF, D), BF),
]


def forward_call(own, recv, gains, mats, rows, seq_count):
    ext = rows + 2 * HALF
    args = ([own] if own is not None else []) + (list(recv) if recv is not None else [])
    shape = jax.ShapeDtypeStruct
    return pl.pallas_call(
        functools.partial(forward_kernel, own is not None, recv is not None, seq_count),
        out_shape=(shape((ext, D), BF), shape((ext, 3 * D), BF), shape((rows, D), BF),
                   shape((rows, D), F32), shape((rows, 2 * FF), F32), shape((rows, D), BF)),
        in_specs=[VM] * (len(args) + 2) + [ANY] * 4,
        out_specs=(VM,) * 6,
        scratch_shapes=WEIGHT_SCRATCH + [pltpu.SemaphoreType.DMA((4,))],
        compiler_params=pltpu.CompilerParams(vmem_limit_bytes=VMEM_LIMIT),
    )(*args, *gains, *mats)


def backward_kernel(has_cot, has_recv, same, seq_count, *refs):
    refs = list(refs)
    cot = refs.pop(0) if has_cot else None
    recv = [refs.pop(0) for _ in range(3)] if has_recv else None
    gain_a, gain_f = refs[:2]
    weights = refs[2:6]
    refs = refs[6:]
    kept_a, refs = refs[:5], refs[5:]
    kept_b, refs = refs[:5], refs[5:]
    (du_ref, du_b_ref, rim_ref, a_ref, dqkv_ref, o_out, dattn_ref, b_ref, dgu_ref, hid_ref, dff_ref,
     ga_ref, gf_ref) = refs[:13]
    s_qkv, s_out, s_in, s_ff, u_s, qkv_s, h_s, gu_s, dout, do_s, acc, sems = refs[13:]
    kept_s = (u_s, qkv_s, o_out, h_s, gu_s)
    rows = du_ref.shape[0]
    ext = rows + 2 * HALF
    sec = lax.axis_index("section")
    seq_idx = lax.axis_index("seq")

    @pl.when(sec == 0)
    def _():
        for i in (4, 3, 0, 1, 2):
            pltpu.make_async_copy(kept_a[i], kept_s[i], sems.at[4 + i]).start()

    @pl.when(sec != 0)
    def _():
        for i in (4, 3, 0, 1, 2):
            pltpu.make_async_copy(kept_b[i], kept_s[i], sems.at[4 + i]).start()

    kept_copies = [pltpu.make_async_copy(kept_a[i], kept_s[i], sems.at[4 + i]) for i in range(5)]
    copies = [pltpu.make_async_copy(src, dst, sems.at[i]) for i, (src, dst) in
              enumerate(zip(weights, (s_qkv, s_out, s_in, s_ff)))]
    for i in (3, 2, 1, 0):
        copies[i].start()
    if has_recv:
        dout[...] = recv[0][...].astype(F32)
        dout[0:HALF] += recv[1][...].astype(F32)
        dout[rows - HALF:rows] += recv[2][...].astype(F32)
        got = dout[...].astype(BF).astype(F32)
    else:
        got = jnp.zeros((rows, D), F32)
    if has_cot:
        pick = (jnp.zeros((rows, D), jnp.int32) + sec) == 1
        got = jnp.where(pick, cot[...].astype(F32), got)
    dout[...] = got
    dff_ref[...] = got.astype(BF)
    copies[3].wait()
    dhid = dot_nt(dff_ref[...], s_ff[...])
    kept_copies[4].wait()
    gate, up = gu_s[:, :FF], gu_s[:, FF:]
    cdf = 0.5 * (1.0 + lax.erf(gate * 0.7071067811865476))
    act = gate * cdf
    hid_ref[...] = (act * up).astype(BF)
    pdf = jnp.exp(-0.5 * gate * gate) * 0.3989422804014327
    dgu_ref[:, :FF] = (dhid * up * (cdf + gate * pdf)).astype(BF)
    dgu_ref[:, FF:] = (dhid * act).astype(BF)
    copies[2].wait()
    db = dot_nt(dgu_ref[...], s_in[...])
    kept_copies[3].wait()
    n, inv = normed_rows(h_s[...])
    b_ref[...] = (n * gain_f[...]).astype(BF)
    gf_ref[...] = jnp.sum(db * n, axis=0, keepdims=True)
    dout[...] += norm_back(db, n, inv, gain_f[...])
    dattn_ref[...] = dout[...].astype(BF)
    copies[1].wait()
    do_s[...] = dot_nt(dattn_ref[...], s_out[...]).astype(BF)
    kept_copies[0].wait()
    kept_copies[1].wait()
    kept_copies[2].wait()
    acc[...] = jnp.zeros_like(acc)
    dqkv_ref[0:HALF, 0:D] = jnp.zeros((HALF, D), BF)
    dqkv_ref[ext - HALF:ext, 0:D] = jnp.zeros((HALF, D), BF)
    qb = min(rows, 128)
    for start in range(0, rows, qb):
        mask = allowed_mask(qb, start, seq_idx, seq_count, rows)
        span = slice(start, start + qb + 2 * HALF)
        mid = slice(HALF + start, HALF + start + qb)
        for p in range(PAIRS):
            lanes = slice(p * 128, p * 128 + 128)
            klanes = slice(D + p * 128, D + p * 128 + 128)
            vlanes = slice(2 * D + p * 128, 2 * D + p * 128 + 128)
            q2 = two_heads(qkv_s[mid, lanes])
            k = qkv_s[span, klanes]
            v = qkv_s[span, vlanes]
            do2 = two_heads(do_s[start:start + qb, lanes])
            probs = probs_of(q2, k, mask)
            dp = dot_nt(do2, v)
            ds = (probs * (dp - jnp.sum(probs * dp, axis=-1, keepdims=True))).astype(BF)
            dqkv_ref[mid, lanes] = (one_of_two(dot_nn(ds, k)) * SCALE).astype(BF)
            acc[span, lanes] += dot_tn(ds, q2) * SCALE
            acc[span, klanes] += dot_tn(probs.astype(BF), do2)
    dqkv_ref[:, D:] = acc[...].astype(BF)
    copies[0].wait()
    da = dot_nt(dqkv_ref[...], s_qkv[...])
    m, inv_u = normed_rows(u_s[...].astype(F32))
    a_ref[...] = (m * gain_a[...]).astype(BF)
    ga_ref[...] = jnp.sum(da * m, axis=0, keepdims=True)
    du = norm_back(da, m, inv_u, gain_a[...])
    rim_ref[0:HALF] = du[:HALF].astype(BF)
    rim_ref[HALF:2 * HALF] = du[ext - HALF:].astype(BF)
    du_mid = dout[...] + du[HALF:HALF + rows]
    du_ref[...] = du_mid
    du_b_ref[...] = du_mid.astype(BF)


def backward_call(cot, recv, gains, mats, kept_a, kept_b, rows, seq_count):
    ext = rows + 2 * HALF
    args = ([cot] if cot is not None else []) + (list(recv) if recv is not None else [])
    shape = jax.ShapeDtypeStruct
    return pl.pallas_call(
        functools.partial(backward_kernel, cot is not None, recv is not None, False, seq_count),
        out_shape=(shape((rows, D), F32), shape((rows, D), BF), shape((2 * HALF, D), BF), shape((ext, D), BF),
                   shape((ext, 3 * D), BF), shape((rows, D), BF), shape((rows, D), BF),
                   shape((rows, D), BF), shape((rows, 2 * FF), BF), shape((rows, FF), BF),
                   shape((rows, D), BF), shape((1, D), F32), shape((1, D), F32)),
        in_specs=[VM] * (len(args) + 2) + [ANY] * 14,
        out_specs=(VM,) * 13,
        scratch_shapes=WEIGHT_SCRATCH + [
            pltpu.VMEM((ext, D), BF), pltpu.VMEM((ext, 3 * D), BF), pltpu.VMEM((rows, D), F32),
            pltpu.VMEM((rows, 2 * FF), F32), pltpu.VMEM((rows, D), F32), pltpu.VMEM((rows, D), BF),
            pltpu.VMEM((ext, 2 * D), F32), pltpu.SemaphoreType.DMA((9,)),
        ],
        compiler_params=pltpu.CompilerParams(vmem_limit_bytes=VMEM_LIMIT),
    )(*args, *gains, *mats, *kept_a, *kept_b)


PIECES = ((3, 0), (2, 0), (2, 1), (2, 2), (1, 0), (0, 0), (0, 1), (0, 2))
MESH = pl.DeviceIdType.MESH


def remote(src, dst, sems, p, i, axis, target):
    return pltpu.make_async_remote_copy(
        src_ref=src, dst_ref=dst, send_sem=sems.at[p, 2 * i], recv_sem=sems.at[p, 2 * i + 1],
        device_id={axis: target}, device_id_type=MESH)


def signal_to(axis, target):
    pl.semaphore_signal(pltpu.get_barrier_semaphore(), inc=1, device_id={axis: target}, device_id_type=MESH)


def weight_kernel(seq_count, *refs):
    chain = seq_count == 4
    slots = (refs[0:8], refs[8:16], refs[16:24])
    ln_terms = (refs[24:27], refs[27:30])
    outs = refs[30:35]
    bufs = refs[35:43]
    full, from_core, from_y, from_l, from_r, total = (refs[43 + 9 * i:52 + 9 * i] for i in range(6))
    sems, rsems = refs[97:99]
    sec = lax.axis_index("section")
    f = lax.axis_index("fsdp")
    z = lax.axis_index("seq")
    core = lax.rem(f, 2)
    y = f // 2
    sibling = y * 2 + (1 - core)
    across = (1 - y) * 2 + core
    signal_to("fsdp", sibling)
    signal_to("fsdp", across)
    if chain:
        @pl.when(z > 0)
        def _():
            signal_to("seq", z - 1)

        @pl.when(z < seq_count - 1)
        def _():
            signal_to("seq", z + 1)
    order = (6, 7, 4, 5, 2, 3, 0, 1)

    def copy(slot, i, part):
        rows = slots[slot][i].shape[0]
        return pltpu.make_async_copy(slots[slot][i], bufs[i].at[pl.ds(part * rows, rows)],
                                     sems.at[part, i])

    for i in order:
        copy(1, i, 0).start()

        @pl.when(sec == 0)
        def _():
            copy(2, i, 1).start()

        @pl.when(sec != 0)
        def _():
            copy(0, i, 1).start()

    def core_copies(p):
        return [remote(full[p].at[k * 2 + (1 - core)], from_core[p].at[k], rsems, p, k, "fsdp", sibling)
                for k in range(2)]

    def y_copy(p):
        return remote(full[p].at[(1 - y) * 2 + core], from_y[p], rsems, p, 2, "fsdp", across)

    def add_core(p):
        for c in core_copies(p):
            c.wait()
        for k in range(2):
            own = full[p].at[k * 2 + core]
            own[...] = (own[...].astype(F32) + from_core[p][k].astype(F32)).astype(BF)
        y_copy(p).start()

    count = len(PIECES) + 1
    ready = set()
    for p in range(count):
        if p < count - 1:
            w, part = PIECES[p]
            if w not in ready:
                ready.add(w)
                for i in (2 * w, 2 * w + 1):
                    copy(1, i, 0).wait()
                    copy(2, i, 1).wait()
            prod = dot_tn(bufs[2 * w][...], bufs[2 * w + 1][:, part * D:part * D + D]).astype(BF)
            rb = prod.shape[0] // 4
            for k in range(4):
                full[p][k] = prod[k * rb:(k + 1) * rb]
        else:
            both = [jnp.broadcast_to(t[0][...] + t[1][...] + t[2][...], (8, D)) for t in ln_terms]
            both = jnp.concatenate(both, axis=0).astype(BF)
            for k in range(4):
                full[p][k] = both
        if p == 0:
            peers = 2
            if chain:
                peers = 2 + (z + seq_count - 1) // seq_count + (2 * seq_count - 2 - z) // seq_count
            pl.semaphore_wait(pltpu.get_barrier_semaphore(), peers)
        for c in core_copies(p):
            c.start()
        if p > 0:
            add_core(p - 1)
    add_core(count - 1)

    def acc(p):
        return full[p].at[y * 2 + core]

    def store(p, ref):
        if p < count - 1:
            w, part = PIECES[p]
            outs[w][:, part * D:part * D + D] = ref[...]
        else:
            outs[4][...] = ref[...]

    def go_right(p):
        return remote(acc(p), from_l[p], rsems, p, 3, "seq", z + 1)

    def go_left(p):
        return remote(acc(p), from_r[p], rsems, p, 4, "seq", z - 1)

    def total_right(p):
        return remote(total[p], total[p], rsems, p, 5, "seq", z + 1)

    def total_left(p):
        return remote(total[p], total[p], rsems, p, 6, "seq", z - 1)

    def add_from(p, ref):
        mine = acc(p)
        mine[...] = (mine[...].astype(F32) + ref[...].astype(F32)).astype(BF)

    def step_a(p):
        y_copy(p).wait()
        add_from(p, from_y[p])
        if not chain:
            store(p, acc(p))
            return

        @pl.when(z == 0)
        def _():
            go_right(p).start()

        @pl.when(z == 3)
        def _():
            go_left(p).start()

    def step_b(p):
        @pl.when(z == 1)
        def _():
            remote(acc(p), from_l[p], rsems, p, 3, "seq", z - 1).wait_recv()
            add_from(p, from_l[p])
            if p % 2:
                go_right(p).start()

        @pl.when(z == 2)
        def _():
            remote(acc(p), from_r[p], rsems, p, 4, "seq", z + 1).wait_recv()
            add_from(p, from_r[p])
            if p % 2 == 0:
                go_left(p).start()

    def step_c(p):
        if p % 2:
            @pl.when(z == 2)
            def _():
                remote(acc(p), from_l[p], rsems, p, 3, "seq", z - 1).wait_recv()
                add_from(p, from_l[p])
                total[p][...] = acc(p)[...]
                total_left(p).start()
                total_right(p).start()
                store(p, total[p])
        else:
            @pl.when(z == 1)
            def _():
                remote(acc(p), from_r[p], rsems, p, 4, "seq", z + 1).wait_recv()
                add_from(p, from_r[p])
                total[p][...] = acc(p)[...]
                total_left(p).start()
                total_right(p).start()
                store(p, total[p])

    def got_from_left(p):
        remote(total[p], total[p], rsems, p, 5, "seq", z - 1).wait_recv()

    def got_from_right(p):
        remote(total[p], total[p], rsems, p, 6, "seq", z + 1).wait_recv()

    def step_d(p):
        if p % 2:
            @pl.when(z == 1)
            def _():
                got_from_right(p)
                total_left(p).start()
                store(p, total[p])

            @pl.when(z == 3)
            def _():
                got_from_left(p)
                store(p, total[p])
        else:
            @pl.when(z == 2)
            def _():
                got_from_left(p)
                total_right(p).start()
                store(p, total[p])

            @pl.when(z == 0)
            def _():
                got_from_right(p)
                store(p, total[p])

    def step_e(p):
        if p % 2:
            @pl.when(z == 0)
            def _():
                got_from_right(p)
                store(p, total[p])
        else:
            @pl.when(z == 3)
            def _():
                got_from_left(p)
                store(p, total[p])

    steps = (step_a, step_b, step_c, step_d, step_e) if chain else (step_a,)
    for t in range(count + len(steps) - 1):
        for lag, step in enumerate(steps):
            if 0 <= t - lag < count:
                step(t - lag)
    if not chain:
        return
    for p in range(count):
        odd = p % 2

        @pl.when(z == 0)
        def _():
            go_right(p).wait_send()

        @pl.when(z == 3)
        def _():
            go_left(p).wait_send()

        @pl.when(z == 1)
        def _():
            if odd:
                go_right(p).wait_send()
                total_left(p).wait_send()
            else:
                total_left(p).wait_send()
                total_right(p).wait_send()

        @pl.when(z == 2)
        def _():
            if odd:
                total_left(p).wait_send()
                total_right(p).wait_send()
            else:
                go_left(p).wait_send()
                total_right(p).wait_send()


def weight_call(slots, ln_terms, seq_count):
    shape = jax.ShapeDtypeStruct
    blocks = [288 if w == 3 else 192 for w, _ in PIECES] + [16]
    blocks[0] = FF // 4
    scratch = [pltpu.VMEM((2 * x.shape[0], x.shape[1]), BF) for x in slots[0]]
    scratch += [pltpu.VMEM((4, rb, D), BF) for rb in blocks]
    scratch += [pltpu.VMEM((2, rb, D), BF) for rb in blocks]
    for _ in range(4):
        scratch += [pltpu.VMEM((rb, D), BF) for rb in blocks]
    return pl.pallas_call(
        functools.partial(weight_kernel, seq_count),
        out_shape=(shape((D // 4, 3 * D), BF), shape((D // 4, D), BF), shape((D // 4, 2 * FF), BF),
                   shape((FF // 4, D), BF), shape((16, D), BF)),
        in_specs=[ANY] * 24 + [VM] * 6,
        out_specs=(VM,) * 5,
        scratch_shapes=scratch + [pltpu.SemaphoreType.DMA((2, 8)), pltpu.SemaphoreType.DMA((9, 14))],
        compiler_params=pltpu.CompilerParams(vmem_limit_bytes=VMEM_LIMIT, collective_id=1, has_side_effects=True),
    )(*slots[0], *slots[1], *slots[2], *ln_terms)


GATHER = ((0, 0), (0, 1), (0, 2), (1, 0), (2, 0), (2, 1), (2, 2), (3, 0))


def gather_kernel(*refs):
    ins, outs, sems, lsems = refs[0:5], refs[5:10], refs[10], refs[11]
    f = lax.axis_index("fsdp")
    z = lax.axis_index("seq")
    core = lax.rem(f, 2)
    y = f // 2
    sibling = y * 2 + (1 - core)
    across = (1 - y) * 2 + core
    near = z + 1 - 2 * lax.rem(z, 2)
    signal_to("fsdp", sibling)
    signal_to("fsdp", across)
    signal_to("seq", near)
    count = len(GATHER) + 1

    def own(p):
        if p == 0:
            return ins[4]
        w, part = GATHER[p - 1]
        return ins[w].at[:, pl.ds(part * D, D)]

    def place(p, who):
        if p == 0:
            return outs[4].at[who]
        w, part = GATHER[p - 1]
        return outs[w].at[who, :, pl.ds(part * D, D)]

    locals_ = [pltpu.make_async_copy(own(p), place(p, f), lsems.at[p]) for p in range(count)]
    for c in locals_:
        c.start()
    pl.semaphore_wait(pltpu.get_barrier_semaphore(), 3)
    for par in range(2):
        @pl.when(lax.rem(z, 2) == par)
        def _():
            for p in range(par, count, 2):
                remote(own(p), place(p, f), sems, p, 0, "fsdp", across).start()
    for p in range(count):
        remote(own(p), place(p, f), sems, p, 1, "fsdp", sibling).start()

    def z_copy(p):
        return remote(place(p, across), place(p, across), sems, p, 2, "seq", near)

    def forward_copy(p):
        return remote(place(p, across), place(p, across), sems, p, 3, "fsdp", sibling)

    for par in range(2):
        @pl.when(lax.rem(z, 2) == par)
        def _():
            mine = list(range(par, count, 2))
            other = list(range(1 - par, count, 2))
            for j in range(6):
                if j < len(mine):
                    p = mine[j]
                    remote(own(p), place(p, across), sems, p, 0, "fsdp", across).wait_recv()
                    z_copy(p).start()
                    forward_copy(p).start()
                if 1 <= j and j - 1 < len(other):
                    p = other[j - 1]
                    z_copy(p).wait_recv()
                    forward_copy(p).start()
            for p in mine:
                remote(own(p), place(p, f), sems, p, 0, "fsdp", across).wait_send()
                z_copy(p).wait_send()
    for p in range(count):
        locals_[p].wait()
        first = remote(own(p), place(p, f), sems, p, 1, "fsdp", sibling)
        first.wait_send()
        remote(own(p), place(p, sibling), sems, p, 1, "fsdp", sibling).wait_recv()
        forward_copy(p).wait_send()
        opposite = (1 - y) * 2 + (1 - core)
        remote(place(p, across), place(p, opposite), sems, p, 3, "fsdp", sibling).wait_recv()


def gather_call(weights, gains):
    shape = jax.ShapeDtypeStruct
    args = tuple(weights) + (gains,)
    return pl.pallas_call(
        gather_kernel,
        out_shape=tuple(shape((4,) + x.shape, BF) for x in args),
        in_specs=[ANY] * 5,
        out_specs=(ANY,) * 5,
        scratch_shapes=[pltpu.SemaphoreType.DMA((9, 8)), pltpu.SemaphoreType.DMA((9,))],
        compiler_params=pltpu.CompilerParams(collective_id=0, has_side_effects=True),
    )(*args)


def neighbours(seq_count, from_sec, to_sec, by):
    return [(from_sec * seq_count + i, to_sec * seq_count + i + by)
            for i in range(seq_count) if 0 <= i + by < seq_count]


def body(inputs, cotangent, w_qkv, w_attn_out, w_in, w_ff_out, ln_attn, ln_ff):
    sec = lax.axis_index("section")
    seq_count = lax.axis_size("seq")
    rows = inputs.shape[2]
    axes = ("section", "seq")
    x = inputs[:, 0]
    right = [(i, i + 1) for i in range(seq_count - 1)]
    left = [(i + 1, i) for i in range(seq_count - 1)]
    from_left = lax.ppermute(x[:, rows - HALF:], "seq", right)
    from_right = lax.ppermute(x[:, :HALF], "seq", left)
    own = jnp.concatenate([from_left, x, from_right], axis=1)
    lnb = jnp.concatenate([jnp.broadcast_to(ln_attn, (8, D // 4)), jnp.broadcast_to(ln_ff, (8, D // 4))], axis=0)
    lnb = jnp.pad(lnb, ((0, 0), (0, 64)))
    got = gather_call((w_qkv[0], w_attn_out[0], w_in[0], w_ff_out[0]), lnb)
    mats = tuple(g.reshape(-1, g.shape[2]) for g in got[:4])
    gains = (got[4][:, 0, :D // 4].astype(F32).reshape(1, D), got[4][:, 8, :D // 4].astype(F32).reshape(1, D))

    def relay(out):
        return (
            lax.ppermute(out, "section", [(0, 1)]),
            lax.ppermute(out[rows - HALF:], axes, neighbours(seq_count, 0, 1, 1)),
            lax.ppermute(out[:HALF], axes, neighbours(seq_count, 0, 1, -1)),
        )

    def relay_back(du_b, rim):
        return (
            lax.ppermute(du_b, "section", [(1, 0)]),
            lax.ppermute(rim[HALF:], axes, neighbours(seq_count, 1, 0, 1)),
            lax.ppermute(rim[:HALF], axes, neighbours(seq_count, 1, 0, -1)),
        )

    kept0 = forward_call(own[0], None, gains, mats, rows, seq_count)
    kept1 = forward_call(own[1], relay(kept0[5]), gains, mats, rows, seq_count)
    kept2 = forward_call(None, relay(kept1[5]), gains, mats, rows, seq_count)
    kept = [k[:5] for k in (kept0, kept1, kept2)]
    cot = cotangent[:, 0]
    back0 = backward_call(cot[0], None, gains, mats, kept[0], kept[1], rows, seq_count)
    back1 = backward_call(cot[1], relay_back(back0[1], back0[2]), gains, mats, kept[0], kept[2], rows, seq_count)
    back2 = backward_call(None, relay_back(back1[1], back1[2]), gains, mats, kept[1], kept[2], rows, seq_count)
    backs = (back0, back1, back2)
    rims = jnp.where(sec == 0, jnp.stack([back1[2], back2[2]]), jnp.stack([back0[2], back1[2]]))
    to_right = lax.ppermute(rims[:, HALF:], "seq", right).astype(F32)
    to_left = lax.ppermute(rims[:, :HALF], "seq", left).astype(F32)
    summed = weight_call([b[3:11] for b in backs], [b[11] for b in backs] + [b[12] for b in backs], seq_count)
    if seq_count != 4:
        summed = lax.psum(tuple(summed), "seq")
    summed = tuple(s.astype(F32) for s in summed)
    g_ln = lax.dynamic_slice_in_dim(summed[4], lax.axis_index("fsdp") * (D // 4), D // 4, axis=1)
    layer_out = jnp.where(sec == 0, jnp.stack([kept0[5], kept1[5]]), jnp.stack([kept1[5], kept2[5]]))
    grad = jnp.where(sec == 0, jnp.stack([back1[0], back2[0]]), jnp.stack([back0[0], back1[0]]))
    pad = ((0, 0), (0, rows - HALF), (0, 0))
    grad = grad + jnp.pad(to_right, pad)
    grad = grad + jnp.pad(to_left, (pad[0], pad[1][::-1], pad[2]))
    grad = jnp.where(sec == 1, grad.astype(BF).astype(F32), grad)
    return (layer_out[None, :, None], grad[None, :, None], summed[0][None], summed[1][None], summed[2][None],
            summed[3][None], g_ln[0:1], g_ln[8:9])


def solution(mesh):
    placed = (
        P(None, "fsdp", "seq", None),
        P(None, "fsdp", "seq", None),
        P("section", "fsdp", None),
        P("section", "fsdp", None),
        P("section", "fsdp", None),
        P("section", "fsdp", None),
        P("section", "fsdp"),
        P("section", "fsdp"),
    )
    return jax.shard_map(
        body,
        mesh=mesh,
        in_specs=placed,
        out_specs=(
            P("section", None, "fsdp", "seq", None),
            P("section", None, "fsdp", "seq", None),
            P("section", "fsdp", None),
            P("section", "fsdp", None),
            P("section", "fsdp", None),
            P("section", "fsdp", None),
            P("section", "fsdp"),
            P("section", "fsdp"),
        ),
        check_vma=False,
    )
```
